32 devices in a mesh: cases: 2 (over y), circ: 4 (over z), width: 4 (over x, core).
Axes of the slice: x: 2, y: 2, z: 4, core: 2. Of those that a mesh axis runs over, the one named last changes fastest.
Arguments:
- forcing: float32 [3, 12, 64, 512], P(None, 'cases', 'width', 'circ'), parts along dimension 1, may hold values from -120 to 120
- case_ids: int32 [2], P('cases'), parts along dimension 0, may hold values from 0 to 15
- load_gain: float32 [16, 3], replicated, may hold values from 0.1 to 1.9
- stiffness: float32 [6, 64, 512], P(None, 'width', 'circ'), may hold values from 0.6 to 1.6
- convection: float32 [6, 64, 512], P(None, 'width', 'circ'), may hold values from 0.5 to 3
- labels: int32 [6, 64], P(None, 'width'), may hold values from 0 to 7
- zone_diagonal: float32 [8, 3, 3], replicated, may hold values from -2 to 2
- zone_coupling: float32 [8, 6, 3, 3], replicated, may hold values from -0.25 to 0.75
- zone_jacobi: float32 [8, 3, 3], replicated, may hold values from -0.03 to 0.18
- coarse_inverse: float32 [12, 12], replicated, may hold values from -4.0690104e-07 to 8.138021e-06
Outputs:
- adjoint_field: float32 [3, 12, 64, 512], P(None, 'cases', 'width', 'circ'), parts along dimension 1
- adjoint_residual: float32 [3, 12, 64, 512], P(None, 'cases', 'width', 'circ'), parts along dimension 1
The draws below stay inside these ranges and needn't reach their ends.
There are 2 independent parts, one for each index of `cases`. The reference program is written for one: setup_inputs(seed, part) draws one part's arguments, and reference() takes and returns one part's arrays. A program takes and returns all parts, laid end to end along the dimension named above; an argument that names none is the same for every part. Nothing has to cross between parts.
All inputs are finite; a program needn't handle non-finite values.
Results may differ from the reference program's by a relative error of at most 0.0003.
Values sent between devices are 32-bit elements; how exact they have to be, the bound alone decides.
A program may use at most 64 MiB of HBM per device.

```python
import math
import jax
import jax.numpy as jnp
from jax import lax

CC = 128
NR = 6
ZONES = 8
LOADS = 16
ITERS = 4
NC = 512
NW = 64
SECTORS = 4
SECTOR_CELLS = 49152


def draw_forcing(key, part):
    key = jax.random.fold_in(key, 11)
    rough_key, level_key = jax.random.split(key, 2)
    circ_pos = jnp.arange(NC, dtype=jnp.float32) / NC
    tread_pos = jnp.arange(NW, dtype=jnp.float32) / NW
    amplitude = (1.0 + 2.0 * circ_pos)[None, None, None, :] * (0.7 + 0.7 * tread_pos)[None, None, :, None]
    sectors = NC // CC
    rough_part = jax.random.truncated_normal(rough_key, -6.0, 6.0, (3, NR, NW, NC), jnp.float32)
    sector_level = jax.random.uniform(level_key, (3, sectors), jnp.float32, -1.5, 1.5)
    spread_level = jnp.repeat(sector_level, CC, axis=1)
    return 2.0 * rough_part * amplitude + spread_level[:, None, None, :]


def draw_zone_coupling(key, part):
    key = jax.random.fold_in(key, 12)
    noise = jax.random.uniform(key, (ZONES, 6, 3, 3), jnp.float32, -0.25, 0.25)
    return 0.5 * jnp.eye(3, dtype=jnp.float32) + noise


def draw_zone_jacobi(key, part):
    key = jax.random.fold_in(key, 13)
    noise = jax.random.uniform(key, (ZONES, 3, 3), jnp.float32, -0.03, 0.03)
    return jnp.eye(3, dtype=jnp.float32) / 7.0 + noise


def draw_coarse_inverse(key, part):
    key = jax.random.fold_in(key, 14)
    diag_key, off_key = jax.random.split(key)
    order = 3 * SECTORS
    identity = jnp.eye(order, dtype=jnp.float32)
    diag_values = jnp.exp(jax.random.uniform(diag_key, (order,), jnp.float32, math.log(0.1), math.log(0.4)))
    off_values = jax.random.uniform(off_key, (order, order), jnp.float32, -0.02, 0.02)
    return (off_values * (1.0 - identity) + identity * diag_values[None, :]) / SECTOR_CELLS


def with_ends(array, stream_key, least, high):
    longest = array.shape.index(max(array.shape))
    spots = []
    for shift in (0, 1):
        where = [jax.random.randint(jax.random.fold_in(stream_key, axis), (), 0, length) for axis, length in enumerate(array.shape)]
        where[longest] = (where[longest] + shift) % array.shape[longest]
        spots.append(tuple(where))
    return array.at[spots[0]].set(least).at[spots[1]].set(high)


def block_levels(own_key, dims, cuts, least, high):
    def one(axis_at, shards_of):
        steps = jax.random.uniform(jax.random.fold_in(jax.random.fold_in(own_key, 6), axis_at), (shards_of,), jnp.float32, least / len(cuts), high / len(cuts))
        return jnp.repeat(jnp.exp(steps), dims[axis_at] // shards_of).reshape((-1,) + (1,) * (len(dims) - axis_at - 1))

    factor_of = one(*cuts[0])
    for cut in cuts[1:]:
        factor_of = factor_of * one(*cut)
    return factor_of


def setup_inputs(seed: int = 0, part: int = 0) -> dict:
    arg_keys = jax.random.split(jax.random.key(seed), 11)
    part_splits = jax.random.split(jax.random.fold_in(arg_keys[10], part), 11)
    forcing = draw_forcing(jax.random.fold_in(jax.random.fold_in(arg_keys[10], part), 71), part)
    case_ids = jax.random.randint(part_splits[1], (1,), 0, LOADS).astype(jnp.int32)
    load_gain = jnp.clip(1.0 + 0.18 * jax.random.normal(arg_keys[2], (LOADS, 3), jnp.float32), 0.1, 1.9)
    stiffness = jnp.clip(jnp.exp(math.log(1.6) - 0.98082923 * jax.random.uniform(arg_keys[3], (NR, NW, NC), jnp.float32) ** block_levels(arg_keys[3], (NR, NW, NC), ((1, 4), (2, 4)), -0.2, 0.2)), 0.6, 1.6)
    convection = jnp.clip(jnp.exp(math.log(3.0) - 1.7917595 * jax.random.uniform(arg_keys[4], (NR, NW, NC), jnp.float32) ** block_levels(arg_keys[4], (NR, NW, NC), ((1, 4), (2, 4)), -0.2, 0.2)), 0.5, 3.0)
    labels = with_ends(jax.random.randint(arg_keys[5], (NR, NW), 0, ZONES), jax.random.fold_in(arg_keys[5], 1), 0, ZONES - 1).astype(jnp.int32)
    zone_diagonal = jnp.clip(jax.random.uniform(arg_keys[6], (ZONES, 3, 3), jnp.float32, -2.0, 2.0), -2.0, 2.0)
    zone_coupling = draw_zone_coupling(jax.random.fold_in(arg_keys[10], 71), part)
    zone_jacobi = draw_zone_jacobi(jax.random.fold_in(arg_keys[10], 71), part)
    coarse_inverse = draw_coarse_inverse(jax.random.fold_in(arg_keys[10], 71), part)
    return {"forcing": forcing, "case_ids": case_ids, "load_gain": load_gain, "stiffness": stiffness, "convection": convection, "labels": labels, "zone_diagonal": zone_diagonal, "zone_coupling": zone_coupling, "zone_jacobi": zone_jacobi, "coarse_inverse": coarse_inverse}


highest = lax.Precision.HIGHEST

def shift_down(values, axis):
    widths = [(0, 0)] * values.ndim
    widths[axis] = (1, 0)
    padded = jnp.pad(values, widths)
    return lax.slice_in_dim(padded, 0, values.shape[axis], axis=axis)

def shift_up(values, axis):
    widths = [(0, 0)] * values.ndim
    widths[axis] = (0, 1)
    padded = jnp.pad(values, widths)
    return lax.slice_in_dim(padded, 1, values.shape[axis] + 1, axis=axis)

def zone_fields(labels, zone_diagonal, zone_coupling, zone_jacobi):
    coupling = jnp.moveaxis(zone_coupling[labels], (0, 1), (3, 4))
    diagonal = jnp.moveaxis(zone_diagonal[labels], (0, 1), (2, 3))
    jacobi = jnp.moveaxis(zone_jacobi[labels], (0, 1), (2, 3))
    return (coupling, diagonal, jacobi)

def transposed(vector, stiffness, convection, coupling, diagonal):
    contrib = [stiffness * jnp.einsum('barw,brwc->arwc', coupling[d], vector, precision=highest) for d in range(6)]
    halfway = 0.5 * convection
    contrib[0] = contrib[0] - halfway * vector
    contrib[1] = contrib[1] + halfway * vector
    result = stiffness * (7.0 * vector + jnp.einsum('barw,brwc->arwc', diagonal, vector, precision=highest))
    moved = [jnp.roll(contrib[0], 1, axis=3), jnp.roll(contrib[1], -1, axis=3), shift_down(contrib[2], 2), shift_up(contrib[3], 2), shift_down(contrib[4], 1), shift_up(contrib[5], 1)]
    for piece in moved:
        result = result - piece
    return result

def precondition(vector, stiffness, jacobi, coarse_inverse):
    sectors = coarse_inverse.shape[0] // 3
    blocks = vector.reshape(3, vector.shape[1], vector.shape[2], sectors, -1)
    coarse = lax.optimization_barrier(jnp.sum(blocks, axis=(1, 2, 4)))
    flattened = coarse.T.reshape(-1)
    solved = jnp.dot(coarse_inverse, flattened, precision=highest).reshape(sectors, 3).T
    spread = jnp.repeat(solved, blocks.shape[4], axis=1)
    local_part = jnp.einsum('abrw,brwc->arwc', jacobi, vector, precision=highest) / stiffness
    return local_part + spread[:, None, None, :]

def least_squares(start_size, hessen):
    count = len(hessen)
    rotated = [start_size] + [jnp.zeros((), start_size.dtype) for spare in range(count)]
    rotations = []
    triangle = []
    for j in range(count):
        column = list(hessen[j])
        for i in range(j):
            cosine, sine_value = rotations[i]
            top_entry = column[i]
            low_entry = column[i + 1]
            column[i] = cosine * top_entry + sine_value * low_entry
            column[i + 1] = cosine * low_entry - sine_value * top_entry
        radius = jnp.sqrt(column[j] * column[j] + column[j + 1] * column[j + 1])
        cosine = column[j] / radius
        sine_value = column[j + 1] / radius
        rotations.append((cosine, sine_value))
        column[j] = radius
        carried = rotated[j]
        rotated[j] = cosine * carried
        rotated[j + 1] = -sine_value * carried
        triangle.append(column[:j + 1])
    weights = [None] * count
    for j in reversed(range(count)):
        remainder = rotated[j]
        for k in range(j + 1, count):
            remainder = remainder - triangle[k][j] * weights[k]
        weights[j] = remainder / triangle[j][j]
    return weights

def reference(forcing, case_ids, load_gain, stiffness, convection, labels, zone_diagonal, zone_coupling, zone_jacobi, coarse_inverse):
    load_row = load_gain[case_ids[0]]
    right_side = forcing * load_row[:, None, None, None]
    coupling, diagonal, jacobi = zone_fields(labels, zone_diagonal, zone_coupling, zone_jacobi)
    start_size = jnp.sqrt(jnp.sum(right_side * right_side))
    krylov = [right_side / start_size]
    hessen = []
    for j in range(ITERS):
        candidate = transposed(precondition(krylov[j], stiffness, jacobi, coarse_inverse), stiffness, convection, coupling, diagonal)
        heights = [jnp.sum(krylov[i] * candidate) for i in range(j + 1)]
        for i in range(j + 1):
            candidate = candidate - heights[i] * krylov[i]
        new_height = jnp.sqrt(jnp.sum(candidate * candidate))
        hessen.append(heights + [new_height])
        if j + 1 < ITERS:
            krylov.append(candidate / new_height)
    weights = least_squares(start_size, hessen)
    combined = weights[0] * krylov[0]
    for j in range(1, ITERS):
        combined = combined + weights[j] * krylov[j]
    adjoint_field = precondition(combined, stiffness, jacobi, coarse_inverse)
    adjoint_residual = right_side - transposed(adjoint_field, stiffness, convection, coupling, diagonal)
    return (adjoint_field, adjoint_residual)
```

```python
import functools

import jax
import jax.numpy as jnp
from jax import lax
from jax.experimental import pallas as pl
from jax.experimental.pallas import tpu as pltpu
from jax.sharding import PartitionSpec as P

ITERS = 4
MESH = pl.DeviceIdType.MESH
DIAGONAL = 54
JACOBI = 63
ROWS = 24


def repeat(count, body):
    if count <= 32:
        for step in range(count):
            body(step)
    else:
        lax.fori_loop(0, count, lambda step, carry: (body(step), carry)[1], 0)


def kernel(
    n_circ,
    n_width,
    forcing,
    case_ids,
    load_gain,
    stiffness,
    convection,
    labels,
    table,
    coarse_inverse,
    field_out,
    residual_out,
    coef,
    basis,
    image,
    padded,
    local,
    label_pad,
    solve_rows,
    ghost_x,
    ghost_w,
    stiff_x,
    stiff_w,
    send_dots,
    recv_dots,
    send_circ,
    recv_circ,
    send_width,
    recv_width,
    sem_send_dots,
    sem_recv_dots,
    sem_send_circ,
    sem_recv_circ,
    sem_send_width,
    sem_recv_width,
):
    layers, width, lanes = stiffness.shape
    slabs = 3 * layers
    group = n_circ * n_width
    at_circ = lax.axis_index("circ")
    at_width = lax.axis_index("width")
    me = at_circ * n_width + at_width
    next_circ = lax.rem(at_circ + 1, n_circ)
    prev_circ = lax.rem(at_circ + n_circ - 1, n_circ)
    next_width = lax.rem(at_width + 1, n_width)
    prev_width = lax.rem(at_width + n_width - 1, n_width)

    def other(step):
        place = lax.rem(me + step + 1, group)
        return {"circ": lax.div(place, n_width), "width": lax.rem(place, n_width)}

    barrier = pltpu.get_barrier_semaphore()
    repeat(
        group - 1,
        lambda step: pl.semaphore_signal(
            barrier, inc=1, device_id=other(step), device_id_type=MESH
        ),
    )

    lane = lax.broadcasted_iota(jnp.int32, (width, lanes), 1)
    even = lax.rem(lane, 2) == 0
    first = lane == 0
    last = lane == lanes - 1

    def roll(value, shift):
        return pltpu.roll(value, shift % lanes, 1)

    def splat(row):
        return jnp.broadcast_to(row, (width, lanes))

    def remote(source, target, send_sem, recv_sem, device):
        return pltpu.make_async_remote_copy(
            src_ref=source,
            dst_ref=target,
            send_sem=send_sem,
            recv_sem=recv_sem,
            device_id=device,
            device_id_type=MESH,
        )

    def neighbours(turn):
        rows = pl.ds(0, 64 if turn == 0 else ROWS)
        return [
            remote(
                send_width.at[turn, 0, rows],
                recv_width.at[turn, 0, rows],
                sem_send_width.at[turn, 0],
                sem_recv_width.at[turn, 0],
                {"circ": at_circ, "width": next_width},
            ),
            remote(
                send_width.at[turn, 1, rows],
                recv_width.at[turn, 1, rows],
                sem_send_width.at[turn, 1],
                sem_recv_width.at[turn, 1],
                {"circ": at_circ, "width": prev_width},
            ),
            remote(
                send_circ.at[turn],
                recv_circ.at[turn, 0],
                sem_send_circ.at[turn, 0],
                sem_recv_circ.at[turn, 0],
                {"circ": next_circ, "width": at_width},
            ),
            remote(
                send_circ.at[turn],
                recv_circ.at[turn, 1],
                sem_send_circ.at[turn, 1],
                sem_recv_circ.at[turn, 1],
                {"circ": prev_circ, "width": at_width},
            ),
        ]

    def send_all(turn, rows):
        message = jnp.concatenate(rows, axis=0)
        send_dots[turn] = message
        recv_dots[turn, me] = message
        repeat(
            group - 1,
            lambda step: remote(
                send_dots.at[turn],
                recv_dots.at[turn, me],
                sem_send_dots.at[turn],
                sem_recv_dots.at[turn],
                other(step),
            ).start(),
        )

    def all_wait(sem):
        whole = recv_dots.at[0, pl.ds(0, group - 1)]
        pltpu.make_async_copy(whole, whole, sem).wait()

    def total(values):
        acc = values[0]
        for value in values[1:]:
            acc = acc + value
        acc = acc[:8] + acc[8:]
        return jnp.sum(acc, axis=0, keepdims=True)

    nothing = jnp.zeros((1, lanes), jnp.float32)

    diagonal_mask = lax.broadcasted_iota(jnp.int32, (width, width), 0) == lax.broadcasted_iota(
        jnp.int32, (width, width), 1
    )
    label_all = labels[...].astype(jnp.float32)
    zone_lane = lane.astype(jnp.float32)
    zones = table.shape[0]

    def zone_rows(label):
        onehot = (label == zone_lane).astype(jnp.float32)[:, :zones]
        return jnp.dot(
            onehot, table[...], precision=lax.Precision.HIGHEST, preferred_element_type=jnp.float32
        )

    own_rows = []
    for r in range(layers):
        row = jnp.broadcast_to(label_all[r : r + 1], (width, width))
        column = jnp.sum(jnp.where(diagonal_mask, row, 0.0), axis=1, keepdims=True)
        label = jnp.broadcast_to(column, (width, lanes))
        label_pad[r, 8 : 8 + width] = label
        own_rows.append(zone_rows(label))
        for k in range(9):
            coef[JACOBI + k, r] = splat(own_rows[r][:, JACOBI + k : JACOBI + k + 1])

    def apply_jacobi(r, value):
        out = []
        for a in range(3):
            acc = coef[JACOBI + 3 * a, r] * value[0]
            for b in range(1, 3):
                acc = acc + coef[JACOBI + 3 * a + b, r] * value[b]
            out.append(acc)
        return out

    def pack(acc, index, value):
        return jnp.where(lax.div(lane, 2) == index, roll(value, 2 * index + 1), acc)

    def edges(turn, index, value):
        send_width[turn, 0, pl.ds(index, 1)] = value[width - 1 :]
        send_width[turn, 1, pl.ds(index, 1)] = value[:1]

    case = case_ids[0]
    load = [load_gain[case, a] for a in range(3)]
    sums = [[], [], []]
    packed = jnp.zeros((width, lanes), jnp.float32)
    for r in range(layers):
        value = [forcing[a, r] * load[a] for a in range(3)]
        mapped = apply_jacobi(r, value)
        for a in range(3):
            index = a * layers + r
            basis[0, index] = value[a]
            local[index] = mapped[a]
            sums[a].append(value[a])
            edges(0, index, mapped[a])
            packed = pack(packed, index, mapped[a])
        stiff = stiffness[r]
        ratio = 0.5 * convection[r] / stiff
        label = label_pad[r, 8 : 8 + width]
        packed = pack(packed, slabs + r, stiff)
        packed = pack(packed, slabs + layers + r, ratio)
        for a in range(3):
            edges(0, ROWS + a * layers + r, stiff)
        edges(0, 2 * ROWS + r, label)
    send_circ[0] = packed
    pl.semaphore_wait(barrier, group - 1)
    for copy in neighbours(0):
        copy.start()
    send_all(0, [nothing] * 5 + [total(sums[a]) for a in range(3)])

    for r in range(layers):
        for b in range(3):
            for a in range(3):
                k = 3 * b + a
                for d in (0, 1, 4, 5):
                    coef[9 * d + k, r] = -splat(own_rows[r][:, 9 * d + k : 9 * d + k + 1])
                own = splat(own_rows[r][:, DIAGONAL + k : DIAGONAL + k + 1])
                coef[DIAGONAL + k, r] = own + 7.0 if a == b else own
    order = 3 * n_circ
    for place, sector in enumerate((at_circ, prev_circ, next_circ)):
        for a in range(3):
            for k in range(order):
                scalar = coarse_inverse[sector * 3 + a, k]
                solve_rows[(place * 3 + a) * order + k] = jnp.full((8, lanes), scalar)

    norms = []
    heights = []
    for j in range(ITERS + 1):
        if j < ITERS:
            for copy in neighbours(j):
                copy.wait_recv()
        all_wait(sem_recv_dots.at[j])
        sectors = []
        for k in range(n_circ):
            acc = recv_dots[j, k * n_width]
            for w in range(1, n_width):
                acc = acc + recv_dots[j, k * n_width + w]
            sectors.append(jnp.broadcast_to(jnp.sum(acc, axis=1, keepdims=True), (8, lanes)))
        whole = sectors[0]
        for k in range(1, n_circ):
            whole = whole + sectors[k]

        def everywhere(array, q):
            return jnp.broadcast_to(array[q : q + 1], (8, lanes))

        if j > 0:
            norms.append(everywhere(whole, 4))
            column = [everywhere(whole, i) for i in range(j)]
            heights.append(column)
            shares = [column[i] / norms[i] for i in range(j)]
            wide = [jnp.concatenate([share, share], axis=0) for share in shares]
        else:
            wide = []
        if j == ITERS:
            square = everywhere(whole, 5)
            break

        parts = [everywhere(sectors[k], 5 + a) for k in range(n_circ) for a in range(3)]
        solved = []
        for place in range(3):
            for a in range(3):
                acc = solve_rows[(place * 3 + a) * order] * parts[0]
                for k in range(1, order):
                    acc = acc + solve_rows[(place * 3 + a) * order + k] * parts[k]
                solved.append(jnp.concatenate([acc, acc], axis=0))
        own_y, prev_y, next_y = solved[:3], solved[3:6], solved[6:]

        behind = recv_circ[j, 0]
        ahead = recv_circ[j, 1]
        halo = jnp.where(even, roll(ahead, -1), roll(behind, 1))
        span = 2 * layers
        if j == 0:
            stiff_x[...] = jnp.where(
                lane < span,
                roll(halo, -3 * span),
                jnp.where(lane < 2 * span, roll(halo, -2 * span), roll(halo, -span)),
            )
            for r in range(layers):
                ratio = 0.5 * convection[r] / stiffness[r]
                end = roll(halo, -(2 * (slabs + layers + r) + 1))
                low = jnp.where(first, end, roll(ratio, 1))
                high = jnp.where(last, end, roll(ratio, -1))
                for a in range(3):
                    coef[4 * a, r] = coef[4 * a, r] + low
                    coef[9 + 4 * a, r] = coef[9 + 4 * a, r] - high
        spread = [jnp.where(even, next_y[a], prev_y[a]) for a in range(3)]
        spread = jnp.where(
            lane < span, spread[0], jnp.where(lane < 2 * span, spread[1], spread[2])
        )
        halo = halo + stiff_x[...] * spread
        for i in range(j):
            halo = halo - wide[i] * ghost_x[i]
        ghost_x[j] = halo

        row_at = lax.broadcasted_iota(jnp.int32, (ROWS, lanes), 0)
        tall_y = [jnp.broadcast_to(own_y[a][:1], (ROWS, lanes)) for a in range(3)]
        row_y = jnp.where(
            row_at < layers, tall_y[0], jnp.where(row_at < 2 * layers, tall_y[1], tall_y[2])
        )
        for side in range(2):
            if j == 0:
                stiff_w[side] = recv_width[0, side, ROWS : 2 * ROWS]
                inside = at_width > 0 if side == 0 else at_width < n_width - 1
                end = jnp.where(inside, recv_width[0, side, 2 * ROWS : 2 * ROWS + 8], -1.0)
                for r in range(layers):
                    if side == 0:
                        label_pad[r, 7:8] = end[r : r + 1]
                    else:
                        label_pad[r, 8 + width : 9 + width] = end[r : r + 1]
            halo = recv_width[j, side, :ROWS] + stiff_w[side] * row_y
            for i in range(j):
                halo = halo - jnp.concatenate([shares[i]] * 3, axis=0) * ghost_w[i, side]
            ghost_w[j, side] = halo
            for index in range(slabs):
                if side == 0:
                    padded[j, index, 7:8] = halo[index : index + 1]
                else:
                    padded[j, index, 8 + width : 9 + width] = halo[index : index + 1]
        if j == 0:
            for r in range(layers):
                below = zone_rows(label_pad[r, 7 : 7 + width])
                above = zone_rows(label_pad[r, 9 : 9 + width])
                for k in range(9):
                    coef[18 + k, r] = -splat(below[:, 18 + k : 19 + k])
                    coef[27 + k, r] = -splat(above[:, 27 + k : 28 + k])

        squares = []
        for r in range(layers):
            stiff = stiffness[r]
            for a in range(3):
                index = a * layers + r
                value = local[index] + stiff * own_y[a]
                for i in range(j):
                    value = value - wide[i] * padded[i, index, 8 : 8 + width]
                padded[j, index, 8 : 8 + width] = value
                if j > 0:
                    vector = image[j - 1, index]
                    for i in range(j):
                        vector = vector - wide[i] * basis[i, index]
                    basis[j, index] = vector
                else:
                    vector = basis[0, index]
                squares.append(vector * vector)

        halo = ghost_x[j]
        products = [[] for i in range(j + 1)]
        lengths = []
        sums = [[], [], []]
        packed = jnp.zeros((width, lanes), jnp.float32)
        for r in range(layers):
            terms = []
            for b in range(3):
                index = b * layers + r
                value = padded[j, index, 8 : 8 + width]
                end = roll(halo, -(2 * index + 1))
                terms.append((DIAGONAL, r, b, value))
                terms.append((0, r, b, jnp.where(first, end, roll(value, 1))))
                terms.append((9, r, b, jnp.where(last, end, roll(value, -1))))
                terms.append((18, r, b, padded[j, index, 7 : 7 + width]))
                terms.append((27, r, b, padded[j, index, 9 : 9 + width]))
                if r > 0:
                    terms.append((36, r - 1, b, padded[j, index - 1, 8 : 8 + width]))
                if r < layers - 1:
                    terms.append((45, r + 1, b, padded[j, index + 1, 8 : 8 + width]))
            out = []
            for a in range(3):
                acc = None
                for base, layer, b, value in terms:
                    term = coef[base + 3 * b + a, layer] * value
                    acc = term if acc is None else acc + term
                out.append(acc)
                image[j, a * layers + r] = acc
                for i in range(j + 1):
                    products[i].append(basis[i, a * layers + r] * acc)
                if j == ITERS - 1:
                    lengths.append(acc * acc)
                else:
                    sums[a].append(acc)
            if j < ITERS - 1:
                mapped = apply_jacobi(r, out)
                for a in range(3):
                    index = a * layers + r
                    local[index] = mapped[a]
                    edges(j + 1, index, mapped[a])
                    packed = pack(packed, index, mapped[a])
        if j < ITERS - 1:
            send_circ[j + 1] = packed
            for copy in neighbours(j + 1):
                copy.start()
        rows = [total(product) for product in products]
        rows = rows + [nothing] * (4 - len(rows)) + [total(squares)]
        if j < ITERS - 1:
            rows = rows + [total(sums[a]) for a in range(3)]
        else:
            rows = rows + [total(lengths), nothing, nothing]
        send_all(j + 1, rows)

    sizes = [jnp.sqrt(norm) for norm in norms]
    rest = square
    for i in range(ITERS):
        rest = rest - heights[-1][i] * shares[i]
    rest = jnp.sqrt(jnp.maximum(rest, 0.0))
    rotated = [sizes[0]]
    rotations = []
    triangle = []
    for j in range(ITERS):
        column = [heights[j][i] / (sizes[i] * sizes[j]) for i in range(j + 1)]
        column.append((sizes[j + 1] if j + 1 < ITERS else rest) / sizes[j])
        for i in range(j):
            cosine, sine = rotations[i]
            top, low = column[i], column[i + 1]
            column[i] = cosine * top + sine * low
            column[i + 1] = cosine * low - sine * top
        radius = jnp.sqrt(column[j] * column[j] + column[j + 1] * column[j + 1])
        cosine, sine = column[j] / radius, column[j + 1] / radius
        rotations.append((cosine, sine))
        column[j] = radius
        carried = rotated[j]
        rotated[j] = cosine * carried
        rotated.append(-sine * carried)
        triangle.append(column[: j + 1])
    weights = [None] * ITERS
    for j in reversed(range(ITERS)):
        remainder = rotated[j]
        for k in range(j + 1, ITERS):
            remainder = remainder - triangle[k][j] * weights[k]
        weights[j] = remainder / triangle[j][j]
    wide = [weights[j] / sizes[j] for j in range(ITERS)]
    wide = [jnp.concatenate([weight, weight], axis=0) for weight in wide]
    for r in range(layers):
        inverse = 1.0 / stiffness[r]
        for a in range(3):
            index = a * layers + r
            value = wide[0] * padded[0, index, 8 : 8 + width]
            residual = basis[0, index] - wide[0] * image[0, index]
            for i in range(1, ITERS):
                value = value + wide[i] * padded[i, index, 8 : 8 + width]
                residual = residual - wide[i] * image[i, index]
            field_out[a, r] = value * inverse
            residual_out[a, r] = residual

    for turn in range(ITERS + 1):
        if turn < ITERS:
            for copy in neighbours(turn):
                copy.wait_send()
        all_wait(sem_send_dots.at[turn])


def on_device(
    n_circ,
    n_width,
    forcing,
    case_ids,
    load_gain,
    stiffness,
    convection,
    labels,
    zone_diagonal,
    zone_coupling,
    zone_jacobi,
    coarse_inverse,
):
    zones = zone_coupling.shape[0]
    table = jnp.concatenate(
        [
            zone_coupling.reshape(zones, 54),
            zone_diagonal.reshape(zones, 9),
            zone_jacobi.reshape(zones, 9),
        ],
        axis=1,
    )
    table = jnp.pad(table, ((0, 0), (0, 128 - table.shape[1])))
    layers, width, lanes = stiffness.shape
    slabs = 3 * layers
    group = n_circ * n_width
    f32 = jnp.float32
    in_vmem = pl.BlockSpec(memory_space=pltpu.VMEM)
    in_smem = pl.BlockSpec(memory_space=pltpu.SMEM)
    dma = pltpu.SemaphoreType.DMA
    return pl.pallas_call(
        functools.partial(kernel, n_circ, n_width),
        out_shape=(
            jax.ShapeDtypeStruct(forcing.shape, f32),
            jax.ShapeDtypeStruct(forcing.shape, f32),
        ),
        in_specs=[in_vmem, in_smem, in_smem, in_vmem, in_vmem, in_vmem, in_vmem, in_smem],
        out_specs=(in_vmem, in_vmem),
        scratch_shapes=[
            pltpu.VMEM((72, layers, width, lanes), f32),
            pltpu.VMEM((ITERS, slabs, width, lanes), f32),
            pltpu.VMEM((ITERS, slabs, width, lanes), f32),
            pltpu.VMEM((ITERS, slabs, width + 16, lanes), f32),
            pltpu.VMEM((slabs, width, lanes), f32),
            pltpu.VMEM((layers, width + 16, lanes), f32),
            pltpu.VMEM((9 * 3 * n_circ, 8, lanes), f32),
            pltpu.VMEM((ITERS, width, lanes), f32),
            pltpu.VMEM((ITERS, 2, ROWS, lanes), f32),
            pltpu.VMEM((width, lanes), f32),
            pltpu.VMEM((2, ROWS, lanes), f32),
            pltpu.VMEM((ITERS + 1, 8, lanes), f32),
            pltpu.VMEM((ITERS + 1, group, 8, lanes), f32),
            pltpu.VMEM((ITERS, width, lanes), f32),
            pltpu.VMEM((ITERS, 2, width, lanes), f32),
            pltpu.VMEM((ITERS, 2, 64, lanes), f32),
            pltpu.VMEM((ITERS, 2, 64, lanes), f32),
            dma((ITERS + 1,)),
            dma((ITERS + 1,)),
            dma((ITERS, 2)),
            dma((ITERS, 2)),
            dma((ITERS, 2)),
            dma((ITERS, 2)),
        ],
        compiler_params=pltpu.CompilerParams(
            collective_id=0, has_side_effects=True, vmem_limit_bytes=40 * 1024 * 1024
        ),
    )(forcing, case_ids, load_gain, stiffness, convection, labels, table, coarse_inverse)


def solution(mesh):
    return jax.shard_map(
        functools.partial(on_device, mesh.shape["circ"], mesh.shape["width"]),
        mesh=mesh,
        in_specs=(
            P(None, "cases", "width", "circ"),
            P("cases"),
            P(),
            P(None, "width", "circ"),
            P(None, "width", "circ"),
            P(None, "width"),
            P(),
            P(),
            P(),
            P(),
        ),
        out_specs=(P(None, "cases", "width", "circ"), P(None, "cases", "width", "circ")),
        check_vma=False,
    )
```

```python
import functools

import jax
import jax.numpy as jnp
from jax import lax
from jax.experimental import pallas as pl
from jax.experimental.pallas import tpu as pltpu
from jax.sharding import PartitionSpec as P

ITERS = 4
MESH = pl.DeviceIdType.MESH
DIAGONAL = 54
JACOBI = 63
ROWS = 24


def kernel(
    n_circ,
    n_width,
    forcing_in,
    case_in,
    gain_in,
    stiffness_in,
    convection_in,
    labels_in,
    diagonal_in,
    coupling_in,
    jacobi_in,
    coarse_in,
    field_out,
    residual_out,
    forcing,
    case_ids,
    gain,
    stiffness,
    convection,
    labels,
    zone_diagonal,
    zone_coupling,
    zone_jacobi,
    coarse_inverse,
    sem_load,
    coef,
    basis,
    image,
    padded,
    local,
    label_pad,
    solve_rows,
    ghost_x,
    ghost_w,
    stiff_x,
    stiff_w,
    send_dots,
    recv_dots,
    send_circ,
    recv_circ,
    send_width,
    recv_width,
    sem_send_dots,
    sem_recv_dots,
    sem_send_circ,
    sem_recv_circ,
    sem_send_width,
    sem_recv_width,
):
    layers, width, lanes = stiffness.shape
    slabs = 3 * layers
    group = n_circ * n_width
    at_circ = lax.axis_index("circ")
    at_width = lax.axis_index("width")
    me = at_circ * n_width + at_width
    next_circ = lax.rem(at_circ + 1, n_circ)
    prev_circ = lax.rem(at_circ + n_circ - 1, n_circ)
    next_width = lax.rem(at_width + 1, n_width)
    prev_width = lax.rem(at_width + n_width - 1, n_width)

    def far(count):
        return sorted(range(count), key=lambda d: -min(d, count - d))

    hops = [(d, e) for d in far(n_circ) for e in far(n_width) if d + e > 0]

    def to_others(body):
        if group <= 32:
            for d, e in hops:
                body(
                    {
                        "circ": lax.rem(at_circ + d, n_circ),
                        "width": lax.rem(at_width + e, n_width),
                    }
                )
        else:

            def step(at, carry):
                place = lax.rem(me + at + 1, group)
                body({"circ": lax.div(place, n_width), "width": lax.rem(place, n_width)})
                return carry

            lax.fori_loop(0, group - 1, step, 0)

    barrier = pltpu.get_barrier_semaphore()
    loads = [
        pltpu.make_async_copy(source, target, sem_load.at[i])
        for i, (source, target) in enumerate(
            [
                (labels_in, labels),
                (jacobi_in, zone_jacobi),
                (coupling_in, zone_coupling),
                (diagonal_in, zone_diagonal),
                (case_in, case_ids),
                (gain_in, gain),
                (forcing_in, forcing),
                (stiffness_in, stiffness),
                (convection_in, convection),
                (coarse_in, coarse_inverse),
            ]
        )
    ]
    for copy in loads:
        copy.start()
    to_others(
        lambda device: pl.semaphore_signal(
            barrier, inc=1, device_id=device, device_id_type=MESH
        )
    )
    for copy in loads:
        copy.wait()

    lane = lax.broadcasted_iota(jnp.int32, (width, lanes), 1)
    even = lax.rem(lane, 2) == 0
    first = lane == 0
    last = lane == lanes - 1

    def roll(value, shift):
        return pltpu.roll(value, shift % lanes, 1)

    def splat(row):
        return jnp.broadcast_to(row, (width, lanes))

    def remote(source, target, send_sem, recv_sem, device):
        return pltpu.make_async_remote_copy(
            src_ref=source,
            dst_ref=target,
            send_sem=send_sem,
            recv_sem=recv_sem,
            device_id=device,
            device_id_type=MESH,
        )

    def neighbours(turn):
        rows = pl.ds(0, 64 if turn == 0 else ROWS)
        return [
            remote(
                send_width.at[turn, 0, rows],
                recv_width.at[turn, 0, rows],
                sem_send_width.at[turn, 0],
                sem_recv_width.at[turn, 0],
                {"circ": at_circ, "width": next_width},
            ),
            remote(
                send_width.at[turn, 1, rows],
                recv_width.at[turn, 1, rows],
                sem_send_width.at[turn, 1],
                sem_recv_width.at[turn, 1],
                {"circ": at_circ, "width": prev_width},
            ),
            remote(
                send_circ.at[turn],
                recv_circ.at[turn, 0],
                sem_send_circ.at[turn, 0],
                sem_recv_circ.at[turn, 0],
                {"circ": next_circ, "width": at_width},
            ),
            remote(
                send_circ.at[turn],
                recv_circ.at[turn, 1],
                sem_send_circ.at[turn, 1],
                sem_recv_circ.at[turn, 1],
                {"circ": prev_circ, "width": at_width},
            ),
        ]

    def send_all(turn, rows):
        message = jnp.concatenate(rows, axis=0)
        send_dots[turn] = message
        recv_dots[turn, me] = message
        to_others(
            lambda device: remote(
                send_dots.at[turn],
                recv_dots.at[turn, me],
                sem_send_dots.at[turn],
                sem_recv_dots.at[turn],
                device,
            ).start()
        )

    def all_wait(sem):
        whole = recv_dots.at[0, pl.ds(0, group - 1)]
        pltpu.make_async_copy(whole, whole, sem).wait()

    def total(values):
        acc = values[0]
        for value in values[1:]:
            acc = acc + value
        acc = acc[:8] + acc[8:]
        return jnp.sum(acc, axis=0, keepdims=True)

    nothing = jnp.zeros((1, lanes), jnp.float32)

    diagonal_mask = lax.broadcasted_iota(jnp.int32, (width, width), 0) == lax.broadcasted_iota(
        jnp.int32, (width, width), 1
    )
    label_all = labels[...].astype(jnp.float32)
    zone_lane = lane.astype(jnp.float32)
    zones, steps = zone_coupling.shape[2:]
    table = jnp.concatenate(
        [zone_coupling[b, a] for b in range(3) for a in range(3)], axis=1
    )

    def zone_rows(label):
        onehot = (label == zone_lane).astype(jnp.float32)[:, :zones]
        return jnp.dot(
            onehot, table, precision=lax.Precision.HIGHEST, preferred_element_type=jnp.float32
        )

    def zone_columns(label, source):
        onehot = (label == zone_lane).astype(jnp.float32)[:, :zones]
        out = []
        for p in range(3):
            rows = lax.dot_general(
                onehot,
                source[p],
                (((1,), (1,)), ((), ())),
                precision=lax.Precision.HIGHEST,
                preferred_element_type=jnp.float32,
            )
            out.extend(splat(rows[:, q : q + 1]) for q in range(3))
        return out

    own_rows = []
    for r in range(layers):
        row = jnp.broadcast_to(label_all[r : r + 1], (width, width))
        column = jnp.sum(jnp.where(diagonal_mask, row, 0.0), axis=1, keepdims=True)
        label = jnp.broadcast_to(column, (width, lanes))
        label_pad[r, 8 : 8 + width] = label
        own_rows.append(zone_rows(label))
        for k, value in enumerate(zone_columns(label, zone_jacobi)):
            coef[JACOBI + k, r] = value

    def apply_jacobi(r, value):
        out = []
        for a in range(3):
            acc = coef[JACOBI + 3 * a, r] * value[0]
            for b in range(1, 3):
                acc = acc + coef[JACOBI + 3 * a + b, r] * value[b]
            out.append(acc)
        return out

    def pack(acc, index, value):
        return jnp.where(lax.div(lane, 2) == index, roll(value, 2 * index + 1), acc)

    def edges(turn, index, value):
        send_width[turn, 0, pl.ds(index, 1)] = value[width - 1 :]
        send_width[turn, 1, pl.ds(index, 1)] = value[:1]

    case = case_ids[0]
    chosen = jnp.where(
        lax.broadcasted_iota(jnp.int32, gain.shape, 1) == case, gain[...], 0.0
    )
    chosen = jnp.sum(chosen, axis=1, keepdims=True)
    load = [jnp.broadcast_to(chosen[a : a + 1], (width, lanes)) for a in range(3)]
    sums = [[], [], []]
    packed = jnp.zeros((width, lanes), jnp.float32)
    for r in range(layers):
        value = [forcing[a, r] * load[a] for a in range(3)]
        mapped = apply_jacobi(r, value)
        for a in range(3):
            index = a * layers + r
            basis[0, index] = value[a]
            local[index] = mapped[a]
            sums[a].append(value[a])
            edges(0, index, mapped[a])
            packed = pack(packed, index, mapped[a])
        stiff = stiffness[r]
        ratio = 0.5 * convection[r] / stiff
        label = label_pad[r, 8 : 8 + width]
        packed = pack(packed, slabs + r, stiff)
        packed = pack(packed, slabs + layers + r, ratio)
        for a in range(3):
            edges(0, ROWS + a * layers + r, stiff)
        edges(0, 2 * ROWS + r, label)
    send_circ[0] = packed
    pl.semaphore_wait(barrier, group - 1)
    for copy in neighbours(0):
        copy.start()
    send_all(0, [nothing] * 5 + [total(sums[a]) for a in range(3)])

    for r in range(layers):
        diagonal = zone_columns(label_pad[r, 8 : 8 + width], zone_diagonal)
        for b in range(3):
            for a in range(3):
                k = 3 * b + a
                for d in (0, 1, 4, 5):
                    coef[9 * d + k, r] = -splat(own_rows[r][:, steps * k + d : steps * k + d + 1])
                own = diagonal[k]
                coef[DIAGONAL + k, r] = own + 7.0 if a == b else own
    order = 3 * n_circ
    for place, sector in enumerate((at_circ, prev_circ, next_circ)):
        for a in range(3):
            row = coarse_inverse[pl.ds(sector * 3 + a, 1)]
            row = jnp.broadcast_to(row, (8, order))
            for k in range(order):
                solve_rows[(place * 3 + a) * order + k] = jnp.broadcast_to(
                    row[:, k : k + 1], (8, lanes)
                )

    norms = []
    heights = []
    for j in range(ITERS + 1):
        if j < ITERS:
            for copy in neighbours(j):
                copy.wait_recv()
        all_wait(sem_recv_dots.at[j])
        sectors = []
        for k in range(n_circ):
            acc = recv_dots[j, k * n_width]
            for w in range(1, n_width):
                acc = acc + recv_dots[j, k * n_width + w]
            sectors.append(jnp.broadcast_to(jnp.sum(acc, axis=1, keepdims=True), (8, lanes)))
        whole = sectors[0]
        for k in range(1, n_circ):
            whole = whole + sectors[k]

        def everywhere(array, q):
            return jnp.broadcast_to(array[q : q + 1], (8, lanes))

        if j > 0:
            norms.append(everywhere(whole, 4))
            column = [everywhere(whole, i) for i in range(j)]
            heights.append(column)
            shares = [column[i] / norms[i] for i in range(j)]
            wide = [jnp.concatenate([share, share], axis=0) for share in shares]
        else:
            wide = []
        if j == ITERS:
            square = everywhere(whole, 5)
            break

        parts = [everywhere(sectors[k], 5 + a) for k in range(n_circ) for a in range(3)]
        solved = []
        for place in range(3):
            for a in range(3):
                acc = solve_rows[(place * 3 + a) * order] * parts[0]
                for k in range(1, order):
                    acc = acc + solve_rows[(place * 3 + a) * order + k] * parts[k]
                solved.append(jnp.concatenate([acc, acc], axis=0))
        own_y, prev_y, next_y = solved[:3], solved[3:6], solved[6:]

        behind = recv_circ[j, 0]
        ahead = recv_circ[j, 1]
        halo = jnp.where(even, roll(ahead, -1), roll(behind, 1))
        span = 2 * layers
        if j == 0:
            stiff_x[...] = jnp.where(
                lane < span,
                roll(halo, -3 * span),
                jnp.where(lane < 2 * span, roll(halo, -2 * span), roll(halo, -span)),
            )
            for r in range(layers):
                ratio = 0.5 * convection[r] / stiffness[r]
                end = roll(halo, -(2 * (slabs + layers + r) + 1))
                low = jnp.where(first, end, roll(ratio, 1))
                high = jnp.where(last, end, roll(ratio, -1))
                for a in range(3):
                    coef[4 * a, r] = coef[4 * a, r] + low
                    coef[9 + 4 * a, r] = coef[9 + 4 * a, r] - high
        spread = [jnp.where(even, next_y[a], prev_y[a]) for a in range(3)]
        spread = jnp.where(
            lane < span, spread[0], jnp.where(lane < 2 * span, spread[1], spread[2])
        )
        halo = halo + stiff_x[...] * spread
        for i in range(j):
            halo = halo - wide[i] * ghost_x[i]
        ghost_x[j] = halo

        row_at = lax.broadcasted_iota(jnp.int32, (ROWS, lanes), 0)
        tall_y = [jnp.broadcast_to(own_y[a][:1], (ROWS, lanes)) for a in range(3)]
        row_y = jnp.where(
            row_at < layers, tall_y[0], jnp.where(row_at < 2 * layers, tall_y[1], tall_y[2])
        )
        for side in range(2):
            if j == 0:
                stiff_w[side] = recv_width[0, side, ROWS : 2 * ROWS]
                inside = at_width > 0 if side == 0 else at_width < n_width - 1
                end = jnp.where(inside, recv_width[0, side, 2 * ROWS : 2 * ROWS + 8], -1.0)
                for r in range(layers):
                    if side == 0:
                        label_pad[r, 7:8] = end[r : r + 1]
                    else:
                        label_pad[r, 8 + width : 9 + width] = end[r : r + 1]
            halo = recv_width[j, side, :ROWS] + stiff_w[side] * row_y
            for i in range(j):
                halo = halo - jnp.concatenate([shares[i]] * 3, axis=0) * ghost_w[i, side]
            ghost_w[j, side] = halo
            for index in range(slabs):
                if side == 0:
                    padded[j, index, 7:8] = halo[index : index + 1]
                else:
                    padded[j, index, 8 + width : 9 + width] = halo[index : index + 1]
        if j == 0:
            for r in range(layers):
                below = zone_rows(label_pad[r, 7 : 7 + width])
                above = zone_rows(label_pad[r, 9 : 9 + width])
                for k in range(9):
                    coef[18 + k, r] = -splat(below[:, steps * k + 2 : steps * k + 3])
                    coef[27 + k, r] = -splat(above[:, steps * k + 3 : steps * k + 4])

        squares = []
        for r in range(layers):
            stiff = stiffness[r]
            for a in range(3):
                index = a * layers + r
                value = local[index] + stiff * own_y[a]
                for i in range(j):
                    value = value - wide[i] * padded[i, index, 8 : 8 + width]
                padded[j, index, 8 : 8 + width] = value
                if j > 0:
                    vector = image[j - 1, index]
                    for i in range(j):
                        vector = vector - wide[i] * basis[i, index]
                    basis[j, index] = vector
                else:
                    vector = basis[0, index]
                squares.append(vector * vector)

        halo = ghost_x[j]
        products = [[] for i in range(j + 1)]
        lengths = []
        sums = [[], [], []]
        packed = jnp.zeros((width, lanes), jnp.float32)
        for r in range(layers):
            terms = []
            for b in range(3):
                index = b * layers + r
                value = padded[j, index, 8 : 8 + width]
                end = roll(halo, -(2 * index + 1))
                terms.append((DIAGONAL, r, b, value))
                terms.append((0, r, b, jnp.where(first, end, roll(value, 1))))
                terms.append((9, r, b, jnp.where(last, end, roll(value, -1))))
                terms.append((18, r, b, padded[j, index, 7 : 7 + width]))
                terms.append((27, r, b, padded[j, index, 9 : 9 + width]))
                if r > 0:
                    terms.append((36, r - 1, b, padded[j, index - 1, 8 : 8 + width]))
                if r < layers - 1:
                    terms.append((45, r + 1, b, padded[j, index + 1, 8 : 8 + width]))
            out = []
            for a in range(3):
                acc = None
                for base, layer, b, value in terms:
                    term = coef[base + 3 * b + a, layer] * value
                    acc = term if acc is None else acc + term
                out.append(acc)
                image[j, a * layers + r] = acc
                for i in range(j + 1):
                    products[i].append(basis[i, a * layers + r] * acc)
                if j == ITERS - 1:
                    lengths.append(acc * acc)
                else:
                    sums[a].append(acc)
            if j < ITERS - 1:
                mapped = apply_jacobi(r, out)
                for a in range(3):
                    index = a * layers + r
                    local[index] = mapped[a]
                    edges(j + 1, index, mapped[a])
                    packed = pack(packed, index, mapped[a])
        if j < ITERS - 1:
            send_circ[j + 1] = packed
            for copy in neighbours(j + 1):
                copy.start()
        rows = [total(product) for product in products]
        rows = rows + [nothing] * (4 - len(rows)) + [total(squares)]
        if j < ITERS - 1:
            rows = rows + [total(sums[a]) for a in range(3)]
        else:
            rows = rows + [total(lengths), nothing, nothing]
        send_all(j + 1, rows)

    sizes = [jnp.sqrt(norm) for norm in norms]
    rest = square
    for i in range(ITERS):
        rest = rest - heights[-1][i] * shares[i]
    rest = jnp.sqrt(jnp.maximum(rest, 0.0))
    rotated = [sizes[0]]
    rotations = []
    triangle = []
    for j in range(ITERS):
        column = [heights[j][i] / (sizes[i] * sizes[j]) for i in range(j + 1)]
        column.append((sizes[j + 1] if j + 1 < ITERS else rest) / sizes[j])
        for i in range(j):
            cosine, sine = rotations[i]
            top, low = column[i], column[i + 1]
            column[i] = cosine * top + sine * low
            column[i + 1] = cosine * low - sine * top
        radius = jnp.sqrt(column[j] * column[j] + column[j + 1] * column[j + 1])
        cosine, sine = column[j] / radius, column[j + 1] / radius
        rotations.append((cosine, sine))
        column[j] = radius
        carried = rotated[j]
        rotated[j] = cosine * carried
        rotated.append(-sine * carried)
        triangle.append(column[: j + 1])
    weights = [None] * ITERS
    for j in reversed(range(ITERS)):
        remainder = rotated[j]
        for k in range(j + 1, ITERS):
            remainder = remainder - triangle[k][j] * weights[k]
        weights[j] = remainder / triangle[j][j]
    wide = [weights[j] / sizes[j] for j in range(ITERS)]
    wide = [jnp.concatenate([weight, weight], axis=0) for weight in wide]
    for r in range(layers):
        inverse = 1.0 / stiffness[r]
        for a in range(3):
            index = a * layers + r
            value = wide[0] * padded[0, index, 8 : 8 + width]
            residual = basis[0, index] - wide[0] * image[0, index]
            for i in range(1, ITERS):
                value = value + wide[i] * padded[i, index, 8 : 8 + width]
                residual = residual - wide[i] * image[i, index]
            field_out[a, r] = value * inverse
            residual_out[a, r] = residual

    for turn in range(ITERS + 1):
        if turn < ITERS:
            for copy in neighbours(turn):
                copy.wait_send()
        all_wait(sem_send_dots.at[turn])


def on_device(
    n_circ,
    n_width,
    forcing,
    case_ids,
    load_gain,
    stiffness,
    convection,
    labels,
    zone_diagonal,
    zone_coupling,
    zone_jacobi,
    coarse_inverse,
):
    operands = [
        forcing,
        case_ids,
        load_gain.T,
        stiffness,
        convection,
        labels,
        zone_diagonal.transpose(1, 2, 0),
        zone_coupling.transpose(2, 3, 0, 1),
        zone_jacobi.transpose(1, 2, 0),
        coarse_inverse,
    ]
    layers, width, lanes = stiffness.shape
    slabs = 3 * layers
    group = n_circ * n_width
    f32 = jnp.float32
    in_vmem = pl.BlockSpec(memory_space=pltpu.VMEM)
    in_hbm = pl.BlockSpec(memory_space=pltpu.HBM)
    dma = pltpu.SemaphoreType.DMA
    operands = [
        operand if i == 1 else pltpu.with_memory_space_constraint(operand, pltpu.HBM)
        for i, operand in enumerate(operands)
    ]
    results = pl.pallas_call(
        functools.partial(kernel, n_circ, n_width),
        out_shape=(
            jax.ShapeDtypeStruct(forcing.shape, f32),
            jax.ShapeDtypeStruct(forcing.shape, f32),
        ),
        in_specs=[in_hbm] * len(operands),
        out_specs=(in_vmem, in_vmem),
        scratch_shapes=[
            (pltpu.SMEM if i == 1 else pltpu.VMEM)(operand.shape, operand.dtype)
            for i, operand in enumerate(operands)
        ]
        + [
            dma((len(operands),)),
            pltpu.VMEM((72, layers, width, lanes), f32),
            pltpu.VMEM((ITERS, slabs, width, lanes), f32),
            pltpu.VMEM((ITERS, slabs, width, lanes), f32),
            pltpu.VMEM((ITERS, slabs, width + 16, lanes), f32),
            pltpu.VMEM((slabs, width, lanes), f32),
            pltpu.VMEM((layers, width + 16, lanes), f32),
            pltpu.VMEM((9 * 3 * n_circ, 8, lanes), f32),
            pltpu.VMEM((ITERS, width, lanes), f32),
            pltpu.VMEM((ITERS, 2, ROWS, lanes), f32),
            pltpu.VMEM((width, lanes), f32),
            pltpu.VMEM((2, ROWS, lanes), f32),
            pltpu.VMEM((ITERS + 1, 8, lanes), f32),
            pltpu.VMEM((ITERS + 1, group, 8, lanes), f32),
            pltpu.VMEM((ITERS, width, lanes), f32),
            pltpu.VMEM((ITERS, 2, width, lanes), f32),
            pltpu.VMEM((ITERS, 2, 64, lanes), f32),
            pltpu.VMEM((ITERS, 2, 64, lanes), f32),
            dma((ITERS + 1,)),
            dma((ITERS + 1,)),
            dma((ITERS, 2)),
            dma((ITERS, 2)),
            dma((ITERS, 2)),
            dma((ITERS, 2)),
        ],
        compiler_params=pltpu.CompilerParams(
            collective_id=0, has_side_effects=True, vmem_limit_bytes=40 * 1024 * 1024
        ),
    )(*operands)
    return results


def solution(mesh):
    return jax.shard_map(
        functools.partial(on_device, mesh.shape["circ"], mesh.shape["width"]),
        mesh=mesh,
        in_specs=(
            P(None, "cases", "width", "circ"),
            P("cases"),
            P(),
            P(None, "width", "circ"),
            P(None, "width", "circ"),
            P(None, "width"),
            P(),
            P(),
            P(),
            P(),
        ),
        out_specs=(P(None, "cases", "width", "circ"), P(None, "cases", "width", "circ")),
        check_vma=False,
    )
```

```python
import functools

import jax
import jax.numpy as jnp
from jax import lax
from jax.experimental import pallas as pl
from jax.experimental.pallas import tpu as pltpu
from jax.sharding import PartitionSpec as P

ITERS = 4
MESH = pl.DeviceIdType.MESH
DIAGONAL = 54
JACOBI = 63
ROWS = 24


def kernel(
    n_circ,
    n_width,
    forcing_in,
    case_in,
    gain_in,
    stiffness_in,
    convection_in,
    labels_in,
    diagonal_in,
    coupling_in,
    jacobi_in,
    coarse_in,
    field_out,
    residual_out,
    forcing,
    case_ids,
    gain,
    stiffness,
    convection,
    labels,
    zone_diagonal,
    zone_coupling,
    zone_jacobi,
    coarse_inverse,
    sem_load,
    coef,
    basis,
    image,
    padded,
    local,
    label_pad,
    solve_rows,
    ghost_x,
    ghost_w,
    stiff_x,
    stiff_w,
    send_dots,
    recv_dots,
    send_circ,
    recv_circ,
    send_width,
    recv_width,
    sem_send_dots,
    sem_recv_dots,
    sem_send_circ,
    sem_recv_circ,
    sem_send_width,
    sem_recv_width,
):
    layers, width, lanes = stiffness.shape
    slabs = 3 * layers
    group = n_circ * n_width
    at_circ = lax.axis_index("circ")
    at_width = lax.axis_index("width")
    me = at_circ * n_width + at_width
    next_circ = lax.rem(at_circ + 1, n_circ)
    prev_circ = lax.rem(at_circ + n_circ - 1, n_circ)
    next_width = lax.rem(at_width + 1, n_width)
    prev_width = lax.rem(at_width + n_width - 1, n_width)

    def far(count):
        return sorted(range(count), key=lambda d: -min(d, count - d))

    hops = [(d, e) for d in far(n_circ) for e in far(n_width) if d + e > 0]

    def to_others(body):
        if group <= 32:
            for d, e in hops:
                body(
                    {
                        "circ": lax.rem(at_circ + d, n_circ),
                        "width": lax.rem(at_width + e, n_width),
                    }
                )
        else:

            def step(at, carry):
                place = lax.rem(me + at + 1, group)
                body({"circ": lax.div(place, n_width), "width": lax.rem(place, n_width)})
                return carry

            lax.fori_loop(0, group - 1, step, 0)

    barrier = pltpu.get_barrier_semaphore()
    loads = [
        pltpu.make_async_copy(source, target, sem_load.at[i])
        for i, (source, target) in enumerate(
            [
                (labels_in, labels),
                (jacobi_in, zone_jacobi),
                (coupling_in, zone_coupling),
                (diagonal_in, zone_diagonal),
                (case_in, case_ids),
                (gain_in, gain),
                (forcing_in, forcing),
                (stiffness_in, stiffness),
                (convection_in, convection),
                (coarse_in, coarse_inverse),
            ]
        )
    ]
    for copy in loads:
        copy.start()
    to_others(
        lambda device: pl.semaphore_signal(
            barrier, inc=1, device_id=device, device_id_type=MESH
        )
    )
    for copy in loads:
        copy.wait()

    lane = lax.broadcasted_iota(jnp.int32, (width, lanes), 1)
    even = lax.rem(lane, 2) == 0
    first = lane == 0
    last = lane == lanes - 1

    def roll(value, shift):
        return pltpu.roll(value, shift % lanes, 1)

    def splat(row):
        return jnp.broadcast_to(row, (width, lanes))

    def remote(source, target, send_sem, recv_sem, device):
        return pltpu.make_async_remote_copy(
            src_ref=source,
            dst_ref=target,
            send_sem=send_sem,
            recv_sem=recv_sem,
            device_id=device,
            device_id_type=MESH,
        )

    def neighbours(turn):
        rows = pl.ds(0, 64 if turn == 0 else ROWS)
        return [
            remote(
                send_width.at[turn, 0, rows],
                recv_width.at[turn, 0, rows],
                sem_send_width.at[turn, 0],
                sem_recv_width.at[turn, 0],
                {"circ": at_circ, "width": next_width},
            ),
            remote(
                send_width.at[turn, 1, rows],
                recv_width.at[turn, 1, rows],
                sem_send_width.at[turn, 1],
                sem_recv_width.at[turn, 1],
                {"circ": at_circ, "width": prev_width},
            ),
            remote(
                send_circ.at[turn],
                recv_circ.at[turn, 0],
                sem_send_circ.at[turn, 0],
                sem_recv_circ.at[turn, 0],
                {"circ": next_circ, "width": at_width},
            ),
            remote(
                send_circ.at[turn],
                recv_circ.at[turn, 1],
                sem_send_circ.at[turn, 1],
                sem_recv_circ.at[turn, 1],
                {"circ": prev_circ, "width": at_width},
            ),
        ]

    def send_all(turn, rows):
        message = jnp.concatenate(rows, axis=0)
        send_dots[turn] = message
        recv_dots[turn, me] = message
        to_others(
            lambda device: remote(
                send_dots.at[turn],
                recv_dots.at[turn, me],
                sem_send_dots.at[turn],
                sem_recv_dots.at[turn],
                device,
            ).start()
        )

    def all_wait(sem):
        whole = recv_dots.at[0, pl.ds(0, group - 1)]
        pltpu.make_async_copy(whole, whole, sem).wait()

    def total(values):
        acc = values[0]
        for value in values[1:]:
            acc = acc + value
        acc = acc[:8] + acc[8:]
        return jnp.sum(acc, axis=0, keepdims=True)

    nothing = jnp.zeros((1, lanes), jnp.float32)

    diagonal_mask = lax.broadcasted_iota(jnp.int32, (width, width), 0) == lax.broadcasted_iota(
        jnp.int32, (width, width), 1
    )
    label_all = labels[...].astype(jnp.float32)
    zone_lane = lane.astype(jnp.float32)
    zones, steps = zone_coupling.shape[2:]
    table = jnp.concatenate(
        [zone_coupling[b, a] for b in range(3) for a in range(3)], axis=1
    )

    def zone_rows(label):
        onehot = (label == zone_lane).astype(jnp.float32)[:, :zones]
        return jnp.dot(
            onehot, table, precision=lax.Precision.HIGHEST, preferred_element_type=jnp.float32
        )

    def zone_columns(label, source):
        onehot = (label == zone_lane).astype(jnp.float32)[:, :zones]
        out = []
        for p in range(3):
            rows = lax.dot_general(
                onehot,
                source[p],
                (((1,), (1,)), ((), ())),
                precision=lax.Precision.HIGHEST,
                preferred_element_type=jnp.float32,
            )
            out.extend(splat(rows[:, q : q + 1]) for q in range(3))
        return out

    own_rows = []
    for r in range(layers):
        row = jnp.broadcast_to(label_all[r : r + 1], (width, width))
        column = jnp.sum(jnp.where(diagonal_mask, row, 0.0), axis=1, keepdims=True)
        label = jnp.broadcast_to(column, (width, lanes))
        label_pad[r, 8 : 8 + width] = label
        own_rows.append(zone_rows(label))
        for k, value in enumerate(zone_columns(label, zone_jacobi)):
            coef[JACOBI + k, r] = value

    def apply_jacobi(r, value):
        out = []
        for a in range(3):
            acc = coef[JACOBI + 3 * a, r] * value[0]
            for b in range(1, 3):
                acc = acc + coef[JACOBI + 3 * a + b, r] * value[b]
            out.append(acc)
        return out

    def pack(acc, index, value):
        return jnp.where(lax.div(lane, 2) == index, roll(value, 2 * index + 1), acc)

    def edges(turn, index, value):
        send_width[turn, 0, pl.ds(index, 1)] = value[width - 1 :]
        send_width[turn, 1, pl.ds(index, 1)] = value[:1]

    case = case_ids[0]
    chosen = jnp.where(
        lax.broadcasted_iota(jnp.int32, gain.shape, 1) == case, gain[...], 0.0
    )
    chosen = jnp.sum(chosen, axis=1, keepdims=True)
    load = [jnp.broadcast_to(chosen[a : a + 1], (width, lanes)) for a in range(3)]
    sums = [[], [], []]
    packed = jnp.zeros((width, lanes), jnp.float32)
    for r in range(layers):
        value = [forcing[a, r] * load[a] for a in range(3)]
        mapped = apply_jacobi(r, value)
        for a in range(3):
            index = a * layers + r
            basis[0, index] = value[a]
            local[index] = mapped[a]
            sums[a].append(value[a])
            edges(0, index, mapped[a])
            packed = pack(packed, index, mapped[a])
        stiff = stiffness[r]
        ratio = 0.5 * convection[r] / stiff
        label = label_pad[r, 8 : 8 + width]
        packed = pack(packed, slabs + r, stiff)
        packed = pack(packed, slabs + layers + r, ratio)
        for a in range(3):
            edges(0, ROWS + a * layers + r, stiff)
        edges(0, 2 * ROWS + r, label)
    send_circ[0] = packed
    pl.semaphore_wait(barrier, group - 1)
    for copy in neighbours(0):
        copy.start()
    send_all(0, [nothing] * 5 + [total(sums[a]) for a in range(3)])

    for r in range(layers):
        diagonal = zone_columns(label_pad[r, 8 : 8 + width], zone_diagonal)
        for b in range(3):
            for a in range(3):
                k = 3 * b + a
                for d in (0, 1, 4, 5):
                    coef[9 * d + k, r] = -splat(own_rows[r][:, steps * k + d : steps * k + d + 1])
                own = diagonal[k]
                coef[DIAGONAL + k, r] = own + 7.0 if a == b else own
    order = 3 * n_circ
    for place, sector in enumerate((at_circ, prev_circ, next_circ)):
        for a in range(3):
            row = coarse_inverse[pl.ds(sector * 3 + a, 1)]
            row = jnp.broadcast_to(row, (8, order))
            for k in range(order):
                solve_rows[(place * 3 + a) * order + k] = jnp.broadcast_to(
                    row[:, k : k + 1], (8, lanes)
                )

    norms = []
    heights = []
    sizes = []
    rotated = []
    rotations = []
    triangle = []

    def rotate(j):
        if j == 0:
            rotated.append(sizes[0])
        column = [heights[j][i] / (sizes[i] * sizes[j]) for i in range(j + 1)]
        column.append(sizes[j + 1] / sizes[j])
        for i in range(j):
            cosine, sine = rotations[i]
            top, low = column[i], column[i + 1]
            column[i] = cosine * top + sine * low
            column[i + 1] = cosine * low - sine * top
        radius = jnp.sqrt(column[j] * column[j] + column[j + 1] * column[j + 1])
        cosine, sine = column[j] / radius, column[j + 1] / radius
        rotations.append((cosine, sine))
        column[j] = radius
        carried = rotated[j]
        rotated[j] = cosine * carried
        rotated.append(-sine * carried)
        triangle.append(column[: j + 1])

    for j in range(ITERS + 1):
        if j < ITERS:
            for copy in neighbours(j):
                copy.wait_recv()
            behind = recv_circ[j, 0]
            ahead = recv_circ[j, 1]
            halo = jnp.where(even, roll(ahead, -1), roll(behind, 1))
            span = 2 * layers
            if j == 0:
                stiff_x[...] = jnp.where(
                    lane < span,
                    roll(halo, -3 * span),
                    jnp.where(lane < 2 * span, roll(halo, -2 * span), roll(halo, -span)),
                )
                for r in range(layers):
                    ratio = 0.5 * convection[r] / stiffness[r]
                    end = roll(halo, -(2 * (slabs + layers + r) + 1))
                    low = jnp.where(first, end, roll(ratio, 1))
                    high = jnp.where(last, end, roll(ratio, -1))
                    for a in range(3):
                        coef[4 * a, r] = coef[4 * a, r] + low
                        coef[9 + 4 * a, r] = coef[9 + 4 * a, r] - high
            if j == 0:
                for side in range(2):
                    stiff_w[side] = recv_width[0, side, ROWS : 2 * ROWS]
                    inside = at_width > 0 if side == 0 else at_width < n_width - 1
                    end = jnp.where(inside, recv_width[0, side, 2 * ROWS : 2 * ROWS + 8], -1.0)
                    for r in range(layers):
                        if side == 0:
                            label_pad[r, 7:8] = end[r : r + 1]
                        else:
                            label_pad[r, 8 + width : 9 + width] = end[r : r + 1]
            if j == 0:
                for r in range(layers):
                    below = zone_rows(label_pad[r, 7 : 7 + width])
                    above = zone_rows(label_pad[r, 9 : 9 + width])
                    for k in range(9):
                        coef[18 + k, r] = -splat(below[:, steps * k + 2 : steps * k + 3])
                        coef[27 + k, r] = -splat(above[:, steps * k + 3 : steps * k + 4])
        all_wait(sem_recv_dots.at[j])
        sectors = []
        for k in range(n_circ):
            acc = recv_dots[j, k * n_width]
            for w in range(1, n_width):
                acc = acc + recv_dots[j, k * n_width + w]
            sectors.append(jnp.broadcast_to(jnp.sum(acc, axis=1, keepdims=True), (8, lanes)))
        whole = sectors[0]
        for k in range(1, n_circ):
            whole = whole + sectors[k]

        def everywhere(array, q):
            return jnp.broadcast_to(array[q : q + 1], (8, lanes))

        if j > 0:
            norms.append(everywhere(whole, 4))
            column = [everywhere(whole, i) for i in range(j)]
            heights.append(column)
            shares = [column[i] / norms[i] for i in range(j)]
            wide = [jnp.concatenate([share, share], axis=0) for share in shares]
        else:
            wide = []
        if j == ITERS:
            square = everywhere(whole, 5)
            break

        parts = [everywhere(sectors[k], 5 + a) for k in range(n_circ) for a in range(3)]
        solved = []
        for place in range(3):
            for a in range(3):
                acc = solve_rows[(place * 3 + a) * order] * parts[0]
                for k in range(1, order):
                    acc = acc + solve_rows[(place * 3 + a) * order + k] * parts[k]
                solved.append(jnp.concatenate([acc, acc], axis=0))
        own_y, prev_y, next_y = solved[:3], solved[3:6], solved[6:]

        spread = [jnp.where(even, next_y[a], prev_y[a]) for a in range(3)]
        spread = jnp.where(
            lane < span, spread[0], jnp.where(lane < 2 * span, spread[1], spread[2])
        )
        halo = halo + stiff_x[...] * spread
        for i in range(j):
            halo = halo - wide[i] * ghost_x[i]
        ghost_x[j] = halo

        row_at = lax.broadcasted_iota(jnp.int32, (ROWS, lanes), 0)
        tall_y = [jnp.broadcast_to(own_y[a][:1], (ROWS, lanes)) for a in range(3)]
        row_y = jnp.where(
            row_at < layers, tall_y[0], jnp.where(row_at < 2 * layers, tall_y[1], tall_y[2])
        )
        for side in range(2):
            halo = recv_width[j, side, :ROWS] + stiff_w[side] * row_y
            for i in range(j):
                halo = halo - jnp.concatenate([shares[i]] * 3, axis=0) * ghost_w[i, side]
            ghost_w[j, side] = halo
            for index in range(slabs):
                if side == 0:
                    padded[j, index, 7:8] = halo[index : index + 1]
                else:
                    padded[j, index, 8 + width : 9 + width] = halo[index : index + 1]
        squares = []
        for r in range(layers):
            stiff = stiffness[r]
            for a in range(3):
                index = a * layers + r
                value = local[index] + stiff * own_y[a]
                for i in range(j):
                    value = value - wide[i] * padded[i, index, 8 : 8 + width]
                padded[j, index, 8 : 8 + width] = value
                if j > 0:
                    vector = image[j - 1, index]
                    for i in range(j):
                        vector = vector - wide[i] * basis[i, index]
                    basis[j, index] = vector
                else:
                    vector = basis[0, index]
                squares.append(vector * vector)

        halo = ghost_x[j]
        products = [[] for i in range(j + 1)]
        lengths = []
        sums = [[], [], []]
        packed = jnp.zeros((width, lanes), jnp.float32)
        for r in range(layers):
            terms = []
            for b in range(3):
                index = b * layers + r
                value = padded[j, index, 8 : 8 + width]
                end = roll(halo, -(2 * index + 1))
                terms.append((DIAGONAL, r, b, value))
                terms.append((0, r, b, jnp.where(first, end, roll(value, 1))))
                terms.append((9, r, b, jnp.where(last, end, roll(value, -1))))
                terms.append((18, r, b, padded[j, index, 7 : 7 + width]))
                terms.append((27, r, b, padded[j, index, 9 : 9 + width]))
                if r > 0:
                    terms.append((36, r - 1, b, padded[j, index - 1, 8 : 8 + width]))
                if r < layers - 1:
                    terms.append((45, r + 1, b, padded[j, index + 1, 8 : 8 + width]))
            out = []
            for a in range(3):
                acc = None
                for base, layer, b, value in terms:
                    term = coef[base + 3 * b + a, layer] * value
                    acc = term if acc is None else acc + term
                out.append(acc)
                image[j, a * layers + r] = acc
                for i in range(j + 1):
                    products[i].append(basis[i, a * layers + r] * acc)
                if j == ITERS - 1:
                    lengths.append(acc * acc)
                else:
                    sums[a].append(acc)
            if j < ITERS - 1:
                mapped = apply_jacobi(r, out)
                for a in range(3):
                    index = a * layers + r
                    local[index] = mapped[a]
                    edges(j + 1, index, mapped[a])
                    packed = pack(packed, index, mapped[a])
        if j < ITERS - 1:
            send_circ[j + 1] = packed
        rows = [total(product) for product in products]
        rows = rows + [nothing] * (4 - len(rows)) + [total(squares)]
        if j < ITERS - 1:
            rows = rows + [total(sums[a]) for a in range(3)]
        else:
            rows = rows + [total(lengths), nothing, nothing]
        send_all(j + 1, rows)
        if j < ITERS - 1:
            for copy in neighbours(j + 1):
                copy.start()
        if j > 0:
            sizes.append(jnp.sqrt(norms[j - 1]))
        if j > 1:
            rotate(j - 2)

    sizes.append(jnp.sqrt(norms[-1]))
    rest = square
    for i in range(ITERS):
        rest = rest - heights[-1][i] * shares[i]
    sizes.append(jnp.sqrt(jnp.maximum(rest, 0.0)))
    for j in range(ITERS - 2, ITERS):
        rotate(j)
    weights = [None] * ITERS
    for j in reversed(range(ITERS)):
        remainder = rotated[j]
        for k in range(j + 1, ITERS):
            remainder = remainder - triangle[k][j] * weights[k]
        weights[j] = remainder / triangle[j][j]
    wide = [weights[j] / sizes[j] for j in range(ITERS)]
    wide = [jnp.concatenate([weight, weight], axis=0) for weight in wide]
    for r in range(layers):
        inverse = 1.0 / stiffness[r]
        for a in range(3):
            index = a * layers + r
            value = wide[0] * padded[0, index, 8 : 8 + width]
            residual = basis[0, index] - wide[0] * image[0, index]
            for i in range(1, ITERS):
                value = value + wide[i] * padded[i, index, 8 : 8 + width]
                residual = residual - wide[i] * image[i, index]
            field_out[a, r] = value * inverse
            residual_out[a, r] = residual

    for turn in range(ITERS + 1):
        if turn < ITERS:
            for copy in neighbours(turn):
                copy.wait_send()
        all_wait(sem_send_dots.at[turn])


def on_device(
    n_circ,
    n_width,
    forcing,
    case_ids,
    load_gain,
    stiffness,
    convection,
    labels,
    zone_diagonal,
    zone_coupling,
    zone_jacobi,
    coarse_inverse,
):
    operands = [
        forcing,
        case_ids,
        load_gain.T,
        stiffness,
        convection,
        labels,
        zone_diagonal.transpose(1, 2, 0),
        zone_coupling.transpose(2, 3, 0, 1),
        zone_jacobi.transpose(1, 2, 0),
        coarse_inverse,
    ]
    layers, width, lanes = stiffness.shape
    slabs = 3 * layers
    group = n_circ * n_width
    f32 = jnp.float32
    in_vmem = pl.BlockSpec(memory_space=pltpu.VMEM)
    in_hbm = pl.BlockSpec(memory_space=pltpu.HBM)
    dma = pltpu.SemaphoreType.DMA
    operands = [
        operand if i == 1 else pltpu.with_memory_space_constraint(operand, pltpu.HBM)
        for i, operand in enumerate(operands)
    ]
    results = pl.pallas_call(
        functools.partial(kernel, n_circ, n_width),
        out_shape=(
            jax.ShapeDtypeStruct(forcing.shape, f32),
            jax.ShapeDtypeStruct(forcing.shape, f32),
        ),
        in_specs=[in_hbm] * len(operands),
        out_specs=(in_vmem, in_vmem),
        scratch_shapes=[
            (pltpu.SMEM if i == 1 else pltpu.VMEM)(operand.shape, operand.dtype)
            for i, operand in enumerate(operands)
        ]
        + [
            dma((len(operands),)),
            pltpu.VMEM((72, layers, width, lanes), f32),
            pltpu.VMEM((ITERS, slabs, width, lanes), f32),
            pltpu.VMEM((ITERS, slabs, width, lanes), f32),
            pltpu.VMEM((ITERS, slabs, width + 16, lanes), f32),
            pltpu.VMEM((slabs, width, lanes), f32),
            pltpu.VMEM((layers, width + 16, lanes), f32),
            pltpu.VMEM((9 * 3 * n_circ, 8, lanes), f32),
            pltpu.VMEM((ITERS, width, lanes), f32),
            pltpu.VMEM((ITERS, 2, ROWS, lanes), f32),
            pltpu.VMEM((width, lanes), f32),
            pltpu.VMEM((2, ROWS, lanes), f32),
            pltpu.VMEM((ITERS + 1, 8, lanes), f32),
            pltpu.VMEM((ITERS + 1, group, 8, lanes), f32),
            pltpu.VMEM((ITERS, width, lanes), f32),
            pltpu.VMEM((ITERS, 2, width, lanes), f32),
            pltpu.VMEM((ITERS, 2, 64, lanes), f32),
            pltpu.VMEM((ITERS, 2, 64, lanes), f32),
            dma((ITERS + 1,)),
            dma((ITERS + 1,)),
            dma((ITERS, 2)),
            dma((ITERS, 2)),
            dma((ITERS, 2)),
            dma((ITERS, 2)),
        ],
        compiler_params=pltpu.CompilerParams(
            collective_id=0, has_side_effects=True, vmem_limit_bytes=40 * 1024 * 1024
        ),
    )(*operands)
    return results


def solution(mesh):
    return jax.shard_map(
        functools.partial(on_device, mesh.shape["circ"], mesh.shape["width"]),
        mesh=mesh,
        in_specs=(
            P(None, "cases", "width", "circ"),
            P("cases"),
            P(),
            P(None, "width", "circ"),
            P(None, "width", "circ"),
            P(None, "width"),
            P(),
            P(),
            P(),
            P(),
        ),
        out_specs=(P(None, "cases", "width", "circ"), P(None, "cases", "width", "circ")),
        check_vma=False,
    )
```
